512 devices in a mesh: context: 64 (over z, y), tensor: 8 (over x, core).
Axes of the slice: x: 4, y: 8, z: 8, core: 2. Of those that a mesh axis runs over, the one named last changes fastest.
Arguments:
- queries: bfloat16 [65536, 2048], P(('context', 'tensor')), may hold values from -6 to 6
- key_rows: bfloat16 [65536, 2048], P(('context', 'tensor')), may hold values from -6 to 6
- value_rows: bfloat16 [65536, 2048], P(('context', 'tensor')), may hold values from -6 to 6
- grad_output: bfloat16 [65536, 2048], P(('context', 'tensor')), may hold values from -6 to 6
Outputs:
- attended: bfloat16 [65536, 2048], P(('context', 'tensor'))
- grad_queries: bfloat16 [65536, 2048], P(('context', 'tensor'))
- grad_keys: bfloat16 [65536, 2048], P(('context', 'tensor'))
- grad_values: bfloat16 [65536, 2048], P(('context', 'tensor'))
The draws below stay inside these ranges and needn't reach their ends.
All inputs are finite; a program needn't handle non-finite values.
Results may differ from the reference program's by a relative error of at most 0.007.
Values may be sent and summed in bfloat16 or wider, within the bound.
A program may use at most 64 MiB of HBM per device.

```python
import jax
import jax.numpy as jnp
from jax import lax

H = 16
DH = 128
TOK_DEV = 128
TOKENS = 65536


def levels(own_key, shape, cuts, smallest, high):
    gain, own = 1.0, jax.random.fold_in(own_key, 6)
    for axis_at, parts in cuts:
        heights = jnp.exp(jax.random.uniform(jax.random.fold_in(own, axis_at), (parts,), jnp.float32, smallest / len(cuts), high / len(cuts)))
        gain = gain * jnp.repeat(heights, shape[axis_at] // parts).reshape([-1 if axis == axis_at else 1 for axis in range(len(shape))])
    return gain


def gaussian(own_key, shape, width, reach, shards=(), held_as=jnp.bfloat16):
    drawn = jax.random.normal(own_key, shape, jnp.float32) * width
    if len(shards) > 0:
        drawn = levels(own_key, shape, shards, -0.22, 0.18) * drawn
    return jnp.clip(drawn, min=-reach, max=reach).astype(held_as)


def setup_inputs(seed: int = 0) -> dict:
    arg_keys = jax.random.split(jax.random.key(seed), 5)
    return {
        "queries": gaussian(arg_keys[0], (TOKENS, H * DH), 1.0, 6.0, ((0, 512),)),
        "key_rows": gaussian(arg_keys[1], (TOKENS, H * DH), 1.0, 6.0, ((0, 512),)),
        "value_rows": gaussian(arg_keys[2], (TOKENS, H * DH), 1.0, 6.0, ((0, 512),)),
        "grad_output": gaussian(arg_keys[3], (TOKENS, H * DH), 1.0, 6.0, ((0, 512),)),
    }


eps = 1e-06

def reference(queries, key_rows, value_rows, grad_output):
    block_rows = TOK_DEV
    blocks_count = TOKENS // block_rows
    precise = lax.Precision.HIGHEST

    def to_blocks(source):
        return source.reshape(blocks_count, block_rows, H, DH)
    query_all = to_blocks(queries)
    key_all = to_blocks(key_rows)
    value_all = to_blocks(value_rows)
    positions = jnp.arange(block_rows, dtype=jnp.int32)
    causal = positions[:, None] >= positions[None, :]
    empty_state = jnp.zeros((H, DH, DH), jnp.float32)

    def forward(state_now, inputs_now):
        query_f = inputs_now[0].astype(jnp.float32)
        key_f = inputs_now[1].astype(jnp.float32)
        value_f = inputs_now[2].astype(jnp.float32)
        scores = jnp.einsum('ihd,jhd->hij', query_f, key_f)
        weights = jnp.where(causal[None], scores, 0.0).astype(jnp.bfloat16)
        attn_out = jnp.einsum('hij,jhd->ihd', weights.astype(jnp.float32), value_f)
        attn_out = attn_out + jnp.einsum('ihd,hde->ihe', query_f, state_now, precision=precise)
        new_state = state_now + jnp.einsum('jhd,jhe->hde', key_f, value_f)
        return (new_state, (attn_out, state_now))
    _, (attn, prefixes) = lax.scan(forward, empty_state, (query_all, key_all, value_all))
    root_mean = jnp.sqrt(lax.optimization_barrier(jnp.mean(attn * attn, axis=-1, keepdims=True)) + eps)
    normed = attn / root_mean
    cotangent = to_blocks(grad_output).astype(jnp.float32)
    d_attn = ((cotangent - normed * lax.optimization_barrier(jnp.mean(cotangent * normed, axis=-1, keepdims=True))) / root_mean).astype(jnp.bfloat16)

    def backward(suffix, inputs_now):
        query_f = inputs_now[0].astype(jnp.float32)
        key_f = inputs_now[1].astype(jnp.float32)
        value_f = inputs_now[2].astype(jnp.float32)
        grad_f = inputs_now[3].astype(jnp.float32)
        state_now = inputs_now[4]
        scores = jnp.einsum('ihd,jhd->hij', query_f, key_f)
        weights = jnp.where(causal[None], scores, 0.0).astype(jnp.bfloat16).astype(jnp.float32)
        d_scores = jnp.einsum('ihd,jhd->hij', grad_f, value_f)
        d_weights = jnp.where(causal[None], d_scores, 0.0).astype(jnp.bfloat16).astype(jnp.float32)
        grad_query = jnp.einsum('hij,jhd->ihd', d_weights, key_f) + jnp.einsum('ihe,hde->ihd', grad_f, state_now, precision=precise)
        grad_key = jnp.einsum('hij,ihd->jhd', d_weights, query_f) + jnp.einsum('jhe,hde->jhd', value_f, suffix, precision=precise)
        grad_value = jnp.einsum('hij,ihd->jhd', weights, grad_f) + jnp.einsum('jhd,hde->jhe', key_f, suffix, precision=precise)
        new_suffix = suffix + jnp.einsum('ihd,ihe->hde', query_f, grad_f)
        return (new_suffix, (grad_query, grad_key, grad_value))
    _, (grad_query, grad_key, grad_value) = lax.scan(backward, empty_state, (query_all, key_all, value_all, d_attn, prefixes), reverse=True)

    def flatten(source):
        return source.reshape(TOKENS, H * DH).astype(jnp.bfloat16)
    return (flatten(normed), flatten(grad_query), flatten(grad_key), flatten(grad_value))
```

```python
import jax
import jax.numpy as jnp
from jax import lax
from jax.experimental import pallas as pl
from jax.experimental.pallas import tpu as pltpu
from jax.sharding import PartitionSpec as P

DH = 128
NZ, NY, NX, NC = 8, 8, 4, 2
STREAMS = 2
EPS = 1e-06
MESH = pl.DeviceIdType.MESH
F32 = jnp.float32
BF16 = jnp.bfloat16


def dot(a, b, ca, cb):
    return lax.dot_general(a, b, (((ca,), (cb,)), ((), ())), preferred_element_type=F32)


def kernel(
    q_in, k_in, v_in, g_in, att_out, gq_out, gk_out, gv_out,
    q, k, v, g, w, local, da, att, gq, gk, gv, gkl, gvl, own_pre,
    cu_s, cu_r, mine, xu_s, xu_r, xpre, yu_s, yu_r, ypre, z_s, z_r,
    yd_s, yd_r, xd_s, xd_r, cd_s, cd_r, ssem, rsem, io_sem,
):
    rows = q.shape[0]
    ctx, ten = lax.axis_index("context"), lax.axis_index("tensor")
    z, y = ctx // NY, lax.rem(ctx, NY)
    x, c = ten // NC, lax.rem(ten, NC)
    peer = 1 - c

    def at_core():
        return (ctx, x * NC + peer)

    def at_x(i):
        return (ctx, i * NC + c)

    def at_y(i):
        return (z * NY + i, ten)

    def at_z(i):
        return (i * NY + y, ten)

    rings = ((at_x, x, NX), (at_y, y, NY), (at_z, z, NZ))
    barrier = pltpu.get_barrier_semaphore()
    pl.semaphore_signal(barrier, inc=1, device_id=at_core(), device_id_type=MESH)
    for place, me, n in rings:
        for off in range(1, n):
            pl.semaphore_signal(
                barrier, inc=1, device_id=place(lax.rem(me + off, n)), device_id_type=MESH
            )

    loads = []
    for i, (src, dst) in enumerate(((k_in, k), (v_in, v), (q_in, q), (g_in, g))):
        loads.append(pltpu.make_async_copy(src, dst, io_sem.at[i]))
        loads[-1].start()

    row_id = lax.broadcasted_iota(jnp.int32, (rows, rows), 0)
    col_id = lax.broadcasted_iota(jnp.int32, (rows, rows), 1)
    causal = row_id >= col_id

    def cols(h):
        return pl.ds(pl.multiple_of(h * DH, DH), DH)

    def head(core, i, s):
        return core * (NX * STREAMS) + i * STREAMS + s

    def copy(src, dst, d, s, r, to):
        return pltpu.make_async_remote_copy(
            src_ref=src, dst_ref=dst, send_sem=ssem.at[d, s, r], recv_sem=rsem.at[d, s, r],
            device_id=to, device_id_type=MESH,
        )

    pending = []

    def scatter(src, dst, d, s, r, ring, whole=False):
        place, me, n = rings[ring]
        for off in range(1, n):
            to = lax.rem(me + off, n)
            copy(src if whole else src.at[to], dst.at[me], d, s, r, place(to)).start()

        def all_of():
            part = dst.at[pl.ds(0, n - 1)]
            return copy(part, part, d, s, r, place(lax.rem(me + 1, n)))

        pending.append(all_of)
        return all_of

    def settle():
        for p in pending:
            p().wait_send()
        pending.clear()

    waits = {}

    def term(d, h):
        if d == 0:
            return dot(k[:, cols(h)], v[:, cols(h)], 0, 0)
        return dot(q[:, cols(h)], da[:, cols(h)], 0, 0)

    def core_up(d, s):
        for i in range(NX):
            cu_s[d, s, i] = term(d, head(peer, i, s)).astype(BF16)
        return lambda: None

    def core_up_send(d, s):
        def whole():
            return copy(cu_s.at[d, s], cu_r.at[d, s], d, s, 0, at_core())

        whole().start()
        pending.append(whole)
        waits[d, s, 0] = whole
        for i in range(NX):
            mine[d, s, i] = term(d, head(c, i, s))

    def x_up(d, s):
        waits[d, s, 0]().wait_recv()
        for i in range(NX):
            xu_s[d, s, i] = (mine[d, s, i] + cu_r[d, s, i].astype(F32)).astype(BF16)
        waits[d, s, 1] = scatter(xu_s.at[d, s], xu_r.at[d, s], d, s, 1, 0)
        xu_r[d, s, x] = xu_s[d, s, x]

    def order(d, n):
        return range(n) if d == 0 else range(n - 1, -1, -1)

    def y_up(d, s):
        waits[d, s, 1]().wait_recv()
        run = jnp.zeros((DH, DH), F32)
        for i in order(d, NX):
            xpre[d, s, i] = run
            run = run + xu_r[d, s, i].astype(F32)
        yu_s[d, s] = run.astype(BF16).reshape(NY, DH // NY, DH)
        waits[d, s, 2] = scatter(yu_s.at[d, s], yu_r.at[d, s], d, s, 2, 1)
        yu_r[d, s, y] = yu_s[d, s, y]

    def z_all(d, s):
        waits[d, s, 2]().wait_recv()
        run = jnp.zeros((DH // NY, DH), F32)
        for i in order(d, NY):
            ypre[d, s, i] = run
            run = run + yu_r[d, s, i].astype(F32)
        z_s[d, s] = run.astype(z_s.dtype)
        waits[d, s, 3] = scatter(z_s.at[d, s], z_r.at[d, s], d, s, 3, 2, whole=True)
        z_r[d, s, z] = z_s[d, s]

    def y_down(d, s):
        waits[d, s, 3]().wait_recv()
        base = jnp.zeros((DH // NY, DH), F32)
        for i in range(NZ):
            passed = i < z if d == 0 else i > z
            base = base + jnp.where(passed, z_r[d, s, i].astype(F32), 0.0)
        for i in range(NY):
            yd_s[d, s, i] = (base + ypre[d, s, i]).astype(BF16)
        waits[d, s, 4] = scatter(yd_s.at[d, s], yd_r.at[d, s], d, s, 4, 1)
        yd_r[d, s, y] = yd_s[d, s, y]

    def x_down(d, s):
        waits[d, s, 4]().wait_recv()
        base = yd_r[d, s].reshape(DH, DH).astype(F32)
        for i in range(NX):
            xd_s[d, s, i] = (base + xpre[d, s, i]).astype(BF16)
        waits[d, s, 5] = scatter(xd_s.at[d, s], xd_r.at[d, s], d, s, 5, 0)
        xd_r[d, s, x] = xd_s[d, s, x]

    def core_down(d, s):
        waits[d, s, 5]().wait_recv()
        first = 0 if d == 0 else 1
        for i in range(NX):
            chip = xd_r[d, s, i].astype(F32)
            cd_s[d, s, i] = (chip + jnp.where(c == first, mine[d, s, i], 0.0)).astype(BF16)
            own_pre[d, s, i] = (
                chip + jnp.where(c == first, 0.0, cu_r[d, s, i].astype(F32))
            ).astype(BF16)

        def whole():
            return copy(cd_s.at[d, s], cd_r.at[d, s], d, s, 6, at_core())

        whole().start()
        pending.append(whole)
        waits[d, s, 6] = whole

    def local_forward(core, s):
        for i in range(NX):
            h = head(core, i, s)
            sc = dot(q[:, cols(h)], k[:, cols(h)], 1, 1)
            wt = jnp.where(causal, sc, 0.0).astype(BF16)
            w[h] = wt
            local[:, cols(h)] = dot(wt, v[:, cols(h)], 1, 0)

    def normalize(core, s, state):
        for i in range(NX):
            h = head(core, i, s)
            a = local[:, cols(h)] + dot(q[:, cols(h)], state[0, s, i], 1, 0)
            inv = lax.rsqrt(jnp.mean(a * a, axis=-1, keepdims=True) + EPS)
            normed = a * inv
            att[:, cols(h)] = normed.astype(BF16)
            cot = g[:, cols(h)].astype(F32)
            m = jnp.mean(cot * normed, axis=-1, keepdims=True)
            da[:, cols(h)] = ((cot - normed * m) * inv).astype(BF16)

    def local_backward(core, s, state):
        for i in range(NX):
            h = head(core, i, s)
            d_a = da[:, cols(h)]
            dw = jnp.where(causal, dot(d_a, v[:, cols(h)], 1, 1), 0.0).astype(BF16)
            gq[:, cols(h)] = (
                dot(dw, k[:, cols(h)], 1, 0) + dot(d_a, state[0, s, i], 1, 1)
            ).astype(BF16)
            gkl[:, cols(h)] = dot(dw, q[:, cols(h)], 0, 0)
            gvl[:, cols(h)] = dot(w[h], d_a, 0, 0)

    def finish(core, s, state):
        for i in range(NX):
            h = head(core, i, s)
            suf = state[1, s, i]
            gk[:, cols(h)] = (gkl[:, cols(h)] + dot(v[:, cols(h)], suf, 1, 1)).astype(BF16)
            gv[:, cols(h)] = (gvl[:, cols(h)] + dot(k[:, cols(h)], suf, 1, 0)).astype(BF16)

    streams = range(STREAMS)
    middle = (x_up, y_up, z_all, y_down, x_down, core_down)

    loads[0].wait()
    loads[1].wait()
    for s in streams:
        core_up(0, s)
        if s == 0:
            pl.semaphore_wait(barrier, 1 + (NX - 1) + (NY - 1) + (NZ - 1))
        core_up_send(0, s)
    loads[2].wait()
    loads[3].wait()
    work = [(core, s) for s in streams for core in (c, peer)]
    for j, stage in enumerate(middle):
        for s in streams:
            stage(0, s)
        if j < len(work):
            local_forward(*work[j])
    settle()
    for s in streams:
        normalize(c, s, own_pre)
        waits[0, s, 6]().wait_recv()
        normalize(peer, s, cd_r)
        core_up(1, s)
        core_up_send(1, s)
    att_copy = pltpu.make_async_copy(att, att_out, io_sem.at[4])
    att_copy.start()
    for j, stage in enumerate(middle):
        for s in streams:
            stage(1, s)
        if j < len(work):
            core, s = work[j]
            local_backward(core, s, own_pre if core is c else cd_r)
        if j + 1 == len(work):
            gq_copy = pltpu.make_async_copy(gq, gq_out, io_sem.at[5])
            gq_copy.start()
    settle_later = list(pending)
    for s in streams:
        finish(c, s, own_pre)
        waits[1, s, 6]().wait_recv()
        finish(peer, s, cd_r)
    gk_copy = pltpu.make_async_copy(gk, gk_out, io_sem.at[6])
    gv_copy = pltpu.make_async_copy(gv, gv_out, io_sem.at[7])
    gk_copy.start()
    gv_copy.start()
    settle()
    att_copy.wait()
    gq_copy.wait()
    gk_copy.wait()
    gv_copy.wait()


def body(queries, key_rows, value_rows, grad_output):
    rows, feats = queries.shape
    heads = feats // DH
    per = (2, STREAMS)
    full = (rows, feats)
    chunk = DH // NY

    def vm(shape, dtype):
        return pltpu.VMEM(shape, dtype)

    scratch = (
        [vm(full, BF16)] * 4
        + [vm((heads, rows, rows), BF16), vm(full, F32), vm(full, BF16)]
        + [vm(full, BF16)] * 4
        + [vm(full, F32)] * 2
        + [vm(per + (NX, DH, DH), BF16)]
        + [vm(per + (NX, DH, DH), BF16)] * 2
        + [vm(per + (NX, DH, DH), F32)]
        + [vm(per + (NX, DH, DH), BF16)] * 2
        + [vm(per + (NX, DH, DH), F32)]
        + [vm(per + (NY, chunk, DH), BF16)] * 2
        + [vm(per + (NY, chunk, DH), F32)]
        + [vm(per + (chunk, DH), BF16), vm(per + (NZ, chunk, DH), BF16)]
        + [vm(per + (NY, chunk, DH), BF16)] * 2
        + [vm(per + (NX, DH, DH), BF16)] * 4
        + [pltpu.SemaphoreType.DMA(per + (7,))] * 2
        + [pltpu.SemaphoreType.DMA((8,))]
    )
    out = jax.ShapeDtypeStruct(full, BF16)
    return pl.pallas_call(
        kernel,
        out_shape=(out,) * 4,
        in_specs=[pl.BlockSpec(memory_space=pl.ANY)] * 4,
        out_specs=(pl.BlockSpec(memory_space=pl.ANY),) * 4,
        scratch_shapes=scratch,
        compiler_params=pltpu.CompilerParams(
            collective_id=0, has_side_effects=True, vmem_limit_bytes=48 * 1024 * 1024
        ),
        cost_estimate=pl.CostEstimate(
            flops=24 * heads * rows * DH * DH, bytes_accessed=16 * rows * feats,
            transcendentals=rows * heads,
        ),
    )(queries, key_rows, value_rows, grad_output)


def solution(mesh):
    spec = P(("context", "tensor"), None)
    return jax.shard_map(
        body, mesh=mesh, in_specs=(spec,) * 4, out_specs=(spec,) * 4, check_vma=False
    )
```

```python
import jax
import jax.numpy as jnp
from jax import lax
from jax.experimental import pallas as pl
from jax.experimental.pallas import tpu as pltpu
from jax.sharding import PartitionSpec as P

DH = 128
NZ, NY, NX, NC = 8, 8, 4, 2
STREAMS = 2
EPS = 1e-06
MESH = pl.DeviceIdType.MESH
F32 = jnp.float32
BF16 = jnp.bfloat16


def dot(a, b, ca, cb):
    return lax.dot_general(a, b, (((ca,), (cb,)), ((), ())), preferred_element_type=F32)


def kernel(
    q_in, k_in, v_in, g_in, att_out, gq_out, gk_out, gv_out,
    q, k, v, g, w, local, da, att, gq, gk, gv, gkl, gvl, own_pre,
    cu_s, cu_r, mine, xu_s, xu_r, xpre, yu_s, yu_r, ypre, z_s, z_r,
    yd_s, yd_r, xd_s, xd_r, cd_s, cd_r, ssem, rsem, io_sem,
):
    rows = q.shape[0]
    ctx, ten = lax.axis_index("context"), lax.axis_index("tensor")
    z, y = ctx // NY, lax.rem(ctx, NY)
    x, c = ten // NC, lax.rem(ten, NC)
    peer = 1 - c

    def at_core():
        return (ctx, x * NC + peer)

    def at_x(i):
        return (ctx, i * NC + c)

    def at_y(i):
        return (z * NY + i, ten)

    def at_z(i):
        return (i * NY + y, ten)

    half = q.shape[1] // NC

    def side(core):
        return pl.ds(pl.multiple_of(core * half, half), half)

    loads = []
    for core in (peer, c):
        for src, dst in ((k_in, k), (v_in, v)):
            loads.append((src.at[:, side(core)], dst.at[:, side(core)]))
    loads += [(q_in, q), (g_in, g)]
    loads = [pltpu.make_async_copy(*pair, io_sem.at[i]) for i, pair in enumerate(loads)]
    for load in loads:
        load.start()

    rings = ((at_x, x, NX), (at_y, y, NY), (at_z, z, NZ))
    barrier = pltpu.get_barrier_semaphore()
    for place, me, n in rings[::-1]:
        for off in sorted(range(1, n), key=lambda step: abs(step - n // 2)):
            pl.semaphore_signal(
                barrier, inc=1, device_id=place(lax.rem(me + off, n)), device_id_type=MESH
            )
    pl.semaphore_signal(barrier, inc=1, device_id=at_core(), device_id_type=MESH)

    row_id = lax.broadcasted_iota(jnp.int32, (rows, rows), 0)
    col_id = lax.broadcasted_iota(jnp.int32, (rows, rows), 1)
    causal = row_id >= col_id

    def cols(h):
        return pl.ds(pl.multiple_of(h * DH, DH), DH)

    def head(core, i, s):
        return core * (NX * STREAMS) + i * STREAMS + s

    def copy(src, dst, d, s, r, to):
        return pltpu.make_async_remote_copy(
            src_ref=src, dst_ref=dst, send_sem=ssem.at[d, s, r], recv_sem=rsem.at[d, s, r],
            device_id=to, device_id_type=MESH,
        )

    pending = []

    def scatter(src, dst, d, s, r, ring, whole=False):
        place, me, n = rings[ring]
        for off in range(1, n):
            to = lax.rem(me + off, n)
            copy(src if whole else src.at[to], dst.at[me], d, s, r, place(to)).start()

        def all_of():
            part = dst.at[pl.ds(0, n - 1)]
            return copy(part, part, d, s, r, place(lax.rem(me + 1, n)))

        pending.append(all_of)
        return all_of

    waits = {}

    def term(d, h):
        if d == 0:
            return dot(k[:, cols(h)], v[:, cols(h)], 0, 0)
        return dot(q[:, cols(h)], da[:, cols(h)], 0, 0)

    def core_up(d, s):
        for i in range(NX):
            cu_s[d, s, i] = term(d, head(peer, i, s)).astype(BF16)

    def core_up_send(d, s):
        def whole():
            return copy(cu_s.at[d, s], cu_r.at[d, s], d, s, 0, at_core())

        whole().start()
        pending.append(whole)
        waits[d, s, 0] = whole

    def own_terms(d, s):
        for i in range(NX):
            mine[d, s, i] = term(d, head(c, i, s))

    def x_up(d, s):
        waits[d, s, 0]().wait_recv()
        for i in range(NX):
            xu_s[d, s, i] = (mine[d, s, i] + cu_r[d, s, i].astype(F32)).astype(BF16)
        waits[d, s, 1] = scatter(xu_s.at[d, s], xu_r.at[d, s], d, s, 1, 0)
        xu_r[d, s, x] = xu_s[d, s, x]

    def order(d, n):
        return range(n) if d == 0 else range(n - 1, -1, -1)

    def y_up(d, s):
        waits[d, s, 1]().wait_recv()
        terms = [xu_r[d, s, i].astype(F32) for i in range(NX)]
        yu_s[d, s] = sum(terms[1:], terms[0]).astype(BF16).reshape(NY, DH // NY, DH)
        waits[d, s, 2] = scatter(yu_s.at[d, s], yu_r.at[d, s], d, s, 2, 1)
        yu_r[d, s, y] = yu_s[d, s, y]
        run = jnp.zeros((DH, DH), F32)
        for i in order(d, NX):
            xpre[d, s, i] = run
            run = run + xu_r[d, s, i].astype(F32)

    def z_all(d, s):
        waits[d, s, 2]().wait_recv()
        terms = [yu_r[d, s, i].astype(F32) for i in range(NY)]
        z_s[d, s] = sum(terms[1:], terms[0]).astype(z_s.dtype)
        waits[d, s, 3] = scatter(z_s.at[d, s], z_r.at[d, s], d, s, 3, 2, whole=True)
        z_r[d, s, z] = z_s[d, s]
        run = jnp.zeros((DH // NY, DH), F32)
        for i in order(d, NY):
            ypre[d, s, i] = run
            run = run + yu_r[d, s, i].astype(F32)

    def y_down(d, s):
        waits[d, s, 3]().wait_recv()
        base = jnp.zeros((DH // NY, DH), F32)
        for i in range(NZ):
            passed = i < z if d == 0 else i > z
            base = base + jnp.where(passed, z_r[d, s, i].astype(F32), 0.0)
        for i in range(NY):
            yd_s[d, s, i] = (base + ypre[d, s, i]).astype(BF16)
        waits[d, s, 4] = scatter(yd_s.at[d, s], yd_r.at[d, s], d, s, 4, 1)
        yd_r[d, s, y] = yd_s[d, s, y]

    def x_down(d, s):
        waits[d, s, 4]().wait_recv()
        base = yd_r[d, s].reshape(DH, DH).astype(F32)
        for i in range(NX):
            xd_s[d, s, i] = (base + xpre[d, s, i]).astype(BF16)
        waits[d, s, 5] = scatter(xd_s.at[d, s], xd_r.at[d, s], d, s, 5, 0)
        xd_r[d, s, x] = xd_s[d, s, x]

    def core_down(d, s):
        waits[d, s, 5]().wait_recv()
        adds_mine = c == (0 if d == 0 else 1)

        def whole(src=cd_s):
            return copy(src.at[d, s], cd_r.at[d, s], d, s, 6, at_core())

        @pl.when(adds_mine)
        def _():
            for i in range(NX):
                cd_s[d, s, i] = (xd_r[d, s, i].astype(F32) + mine[d, s, i]).astype(BF16)
            whole().start()
            own_pre[d, s] = xd_r[d, s]

        @pl.when(jnp.logical_not(adds_mine))
        def _():
            whole(xd_r).start()
            for i in range(NX):
                own_pre[d, s, i] = (
                    xd_r[d, s, i].astype(F32) + cu_r[d, s, i].astype(F32)
                ).astype(BF16)

        pending.append(whole)
        waits[d, s, 6] = whole

    def local_forward(core, s):
        for i in range(NX):
            h = head(core, i, s)
            sc = dot(q[:, cols(h)], k[:, cols(h)], 1, 1)
            wt = jnp.where(causal, sc, 0.0).astype(BF16)
            w[h] = wt
            local[:, cols(h)] = dot(wt, v[:, cols(h)], 1, 0)

    def normalize(core, s, state):
        for i in range(NX):
            h = head(core, i, s)
            a = local[:, cols(h)] + dot(q[:, cols(h)], state[0, s, i], 1, 0)
            inv = lax.rsqrt(jnp.mean(a * a, axis=-1, keepdims=True) + EPS)
            normed = a * inv
            att[:, cols(h)] = normed.astype(BF16)
            cot = g[:, cols(h)].astype(F32)
            m = jnp.mean(cot * normed, axis=-1, keepdims=True)
            da[:, cols(h)] = ((cot - normed * m) * inv).astype(BF16)

    def local_backward(core, s, state):
        for i in range(NX):
            h = head(core, i, s)
            d_a = da[:, cols(h)]
            dw = jnp.where(causal, dot(d_a, v[:, cols(h)], 1, 1), 0.0).astype(BF16)
            gq[:, cols(h)] = (
                dot(dw, k[:, cols(h)], 1, 0) + dot(d_a, state[0, s, i], 1, 1)
            ).astype(BF16)
            gkl[:, cols(h)] = dot(dw, q[:, cols(h)], 0, 0)
            gvl[:, cols(h)] = dot(w[h], d_a, 0, 0)

    def finish(core, s, state):
        for i in range(NX):
            h = head(core, i, s)
            suf = state[1, s, i]
            gk[:, cols(h)] = (gkl[:, cols(h)] + dot(v[:, cols(h)], suf, 1, 1)).astype(BF16)
            gv[:, cols(h)] = (gvl[:, cols(h)] + dot(k[:, cols(h)], suf, 1, 0)).astype(BF16)

    streams = range(STREAMS)
    middle = (x_up, y_up, z_all, y_down, x_down, core_down)

    loads[0].wait()
    loads[1].wait()
    core_up(0, 0)
    pl.semaphore_wait(barrier, 1 + (NX - 1) + (NY - 1) + (NZ - 1))
    core_up_send(0, 0)
    core_up(0, 1)
    core_up_send(0, 1)
    loads[2].wait()
    loads[3].wait()
    for s in streams:
        own_terms(0, s)
    loads[4].wait()
    loads[5].wait()
    work = [(core, s) for s in streams for core in (c, peer)]
    for j, stage in enumerate(middle):
        for s in streams:
            stage(0, s)
        if j < len(work):
            local_forward(*work[j])
    sent = list(pending)
    for s in streams:
        normalize(c, s, own_pre)
        waits[0, s, 6]().wait_recv()
        normalize(peer, s, cd_r)
        core_up(1, s)
        core_up_send(1, s)
        own_terms(1, s)
    att_copy = pltpu.make_async_copy(att, att_out, io_sem.at[6])
    att_copy.start()
    for j, stage in enumerate(middle):
        for s in streams:
            stage(1, s)
        if j < len(work):
            core, s = work[j]
            local_backward(core, s, own_pre if core is c else cd_r)
        if j + 1 == len(work):
            gq_copy = pltpu.make_async_copy(gq, gq_out, io_sem.at[7])
            gq_copy.start()
            for one in sent:
                one().wait_send()
                pending.remove(one)

    last = []

    def leave(core, at):
        for i, (src, dst) in enumerate(((gk, gk_out), (gv, gv_out))):
            move = pltpu.make_async_copy(
                src.at[:, side(core)], dst.at[:, side(core)], io_sem.at[at + i]
            )
            move.start()
            last.append(move)

    for s in streams:
        finish(c, s, own_pre)
    leave(c, 8)
    for s in streams:
        waits[1, s, 6]().wait_recv()
        finish(peer, s, cd_r)
    leave(peer, 10)
    for one in pending:
        one().wait_send()
    for move in [att_copy, gq_copy] + last:
        move.wait()


def hand_over(a, b, c, d, a_out, b_out, c_out, d_out, sem):
    copies = [
        pltpu.make_async_copy(src, dst, sem.at[i])
        for i, (src, dst) in enumerate(((a, a_out), (b, b_out), (c, c_out), (d, d_out)))
    ]
    for move in copies:
        move.start()
    for move in copies:
        move.wait()


def body(queries, key_rows, value_rows, grad_output):
    rows, feats = queries.shape
    heads = feats // DH
    per = (2, STREAMS)
    full = (rows, feats)
    chunk = DH // NY

    def vm(shape, dtype):
        return pltpu.VMEM(shape, dtype)

    scratch = (
        [vm(full, BF16)] * 4
        + [vm((heads, rows, rows), BF16), vm(full, F32), vm(full, BF16)]
        + [vm(full, BF16)] * 4
        + [vm(full, F32)] * 2
        + [vm(per + (NX, DH, DH), BF16)]
        + [vm(per + (NX, DH, DH), BF16)] * 2
        + [vm(per + (NX, DH, DH), F32)]
        + [vm(per + (NX, DH, DH), BF16)] * 2
        + [vm(per + (NX, DH, DH), F32)]
        + [vm(per + (NY, chunk, DH), BF16)] * 2
        + [vm(per + (NY, chunk, DH), F32)]
        + [vm(per + (chunk, DH), BF16), vm(per + (NZ, chunk, DH), BF16)]
        + [vm(per + (NY, chunk, DH), BF16)] * 2
        + [vm(per + (NX, DH, DH), BF16)] * 4
        + [pltpu.SemaphoreType.DMA(per + (7,))] * 2
        + [pltpu.SemaphoreType.DMA((12,))]
    )
    out = jax.ShapeDtypeStruct(full, BF16)
    results = pl.pallas_call(
        kernel,
        out_shape=(out,) * 4,
        in_specs=[pl.BlockSpec(memory_space=pltpu.HBM)] * 4,
        out_specs=(pl.BlockSpec(memory_space=pl.ANY),) * 4,
        scratch_shapes=scratch,
        compiler_params=pltpu.CompilerParams(
            collective_id=0, has_side_effects=True, vmem_limit_bytes=52864 * 1024
        ),
        cost_estimate=pl.CostEstimate(
            flops=24 * heads * rows * DH * DH, bytes_accessed=16 * rows * feats,
            transcendentals=rows * heads,
        ),
    )(queries, key_rows, value_rows, grad_output)
    return pl.pallas_call(
        hand_over,
        out_shape=(out,) * 4,
        in_specs=[pl.BlockSpec(memory_space=pl.ANY)] * 4,
        out_specs=(pl.BlockSpec(memory_space=pl.ANY),) * 4,
        scratch_shapes=[pltpu.SemaphoreType.DMA((4,))],
        compiler_params=pltpu.CompilerParams(vmem_limit_bytes=8 * 1024 * 1024),
    )(*results)


def solution(mesh):
    spec = P(("context", "tensor"), None)
    return jax.shard_map(
        body, mesh=mesh, in_specs=(spec,) * 4, out_specs=(spec,) * 4, check_vma=False
    )
```

```python
import jax
import jax.numpy as jnp
from jax import lax
from jax.experimental import pallas as pl
from jax.experimental.pallas import tpu as pltpu
from jax.sharding import PartitionSpec as P

DH = 128
NZ, NY, NX, NC = 8, 8, 4, 2
STREAMS = 2
EPS = 1e-06
MESH = pl.DeviceIdType.MESH
F32 = jnp.float32
BF16 = jnp.bfloat16


def dot(a, b, ca, cb):
    return lax.dot_general(a, b, (((ca,), (cb,)), ((), ())), preferred_element_type=F32)


def kernel(
    q_in, k_in, v_in, g_in, att_out, gq_out, gk_out, gv_out,
    q, k, v, g, w, local, da, att, gq, gk, gv, gkl, gvl,
    first_term, second_state, xu_s, xu_r, xpre, yu_s, yu_r, ypre, z_s, z_r,
    yd_s, yd_r, xd_s, xd_r, ssem, rsem, own_sem, far_s, far_r,
):
    rows, half = q.shape[1], q.shape[2]
    part = half // STREAMS
    ctx, ten = lax.axis_index("context"), lax.axis_index("tensor")
    z, y = ctx // NY, lax.rem(ctx, NY)
    x, c = ten // NC, lax.rem(ten, NC)
    peer = 1 - c
    to_peer = (ctx, x * NC + peer)
    streams = range(STREAMS)

    def at_x(i):
        return (ctx, i * NC + c)

    def at_y(i):
        return (z * NY + i, ten)

    def at_z(i):
        return (i * NY + y, ten)

    def span(core, s):
        if s is None:
            return pl.ds(pl.multiple_of(core * half, half), half)
        return pl.ds(pl.multiple_of(core * half + s * part, part), part)

    def within(s):
        return pl.ds(0, half) if s is None else pl.ds(s * part, part)

    def near(i, src, dst):
        return pltpu.make_async_copy(src, dst, own_sem.at[i])

    def far(i, src, dst):
        return pltpu.make_async_remote_copy(
            src_ref=src, dst_ref=dst, send_sem=far_s.at[i], recv_sem=far_r.at[i],
            device_id=to_peer, device_id_type=MESH,
        )

    entering = [(k_in, k, 0), (v_in, v, 0), (k_in, k, 1), (v_in, v, 1), (q_in, q, None), (g_in, g, None)]
    own_in = [
        near(i, src.at[:, span(c, s)], dst.at[c, :, within(s)])
        for i, (src, dst, s) in enumerate(entering)
    ]
    far_in = [
        far(i, src.at[:, span(peer, s)], dst.at[c, :, within(s)])
        for i, (src, dst, s) in enumerate(entering)
    ]
    for move in own_in:
        move.start()

    rings = ((at_x, x, NX), (at_y, y, NY), (at_z, z, NZ))
    barrier = pltpu.get_barrier_semaphore()
    pl.semaphore_signal(barrier, inc=1, device_id=to_peer, device_id_type=MESH)
    for place, me, n in rings[::-1]:
        for off in sorted(range(1, n), key=lambda step: abs(step - n // 2)):
            pl.semaphore_signal(
                barrier, inc=1, device_id=place(lax.rem(me + off, n)), device_id_type=MESH
            )

    row_id = lax.broadcasted_iota(jnp.int32, (rows, rows), 0)
    col_id = lax.broadcasted_iota(jnp.int32, (rows, rows), 1)
    causal = row_id >= col_id

    def cols(h):
        return pl.ds(pl.multiple_of(h * DH, DH), DH)

    def copy(src, dst, d, s, r, to):
        return pltpu.make_async_remote_copy(
            src_ref=src, dst_ref=dst, send_sem=ssem.at[d, s, r], recv_sem=rsem.at[d, s, r],
            device_id=to, device_id_type=MESH,
        )

    pending = []
    waits = {}

    def expect(dst, d, s, r, ring):
        place, me, n = rings[ring]

        def all_of():
            slots = dst.at[pl.ds(0, n - 1)]
            return copy(slots, slots, d, s, r, place(lax.rem(me + 1, n)))

        pending.append(all_of)
        waits[d, s, r] = all_of

    def scatter(src, dst, d, s, r, ring, whole=False):
        place, me, n = rings[ring]
        for off in range(1, n):
            to = lax.rem(me + off, n)
            copy(src if whole else src.at[to], dst.at[me], d, s, r, place(to)).start()
        expect(dst, d, s, r, ring)

    def order(d, n):
        return range(n) if d == 0 else range(n - 1, -1, -1)

    def x_up(d, s):
        left, right = (k, v) if d == 0 else (q, da)
        for off in list(range(1, NX)) + [0]:
            i = lax.rem(x + off, NX)
            at = cols(s * NX + i)
            ones = [dot(left[b, :, at], right[b, :, at], 0, 0) for b in order(d, NC)]
            total = (ones[0] + ones[1]).astype(BF16)
            if off:
                xu_s[d, s, i] = total
                copy(xu_s.at[d, s, i], xu_r.at[d, s, x], d, s, 0, at_x(i)).start()
            else:
                xu_r[d, s, x] = total
            first_term[d, s, i] = ones[0]
        expect(xu_r.at[d, s], d, s, 0, 0)

    def y_up(d, s):
        waits[d, s, 0]().wait_recv()
        terms = [xu_r[d, s, i].astype(F32) for i in range(NX)]
        yu_s[d, s] = sum(terms[1:], terms[0]).astype(BF16).reshape(NY, DH // NY, DH)
        scatter(yu_s.at[d, s], yu_r.at[d, s], d, s, 1, 1)
        yu_r[d, s, y] = yu_s[d, s, y]
        run = jnp.zeros((DH, DH), F32)
        for i in order(d, NX):
            xpre[d, s, i] = run
            run = run + xu_r[d, s, i].astype(F32)

    def z_all(d, s):
        waits[d, s, 1]().wait_recv()
        terms = [yu_r[d, s, i].astype(F32) for i in range(NY)]
        z_s[d, s] = sum(terms[1:], terms[0]).astype(z_s.dtype)
        scatter(z_s.at[d, s], z_r.at[d, s], d, s, 2, 2, whole=True)
        z_r[d, s, z] = z_s[d, s]
        run = jnp.zeros((DH // NY, DH), F32)
        for i in order(d, NY):
            ypre[d, s, i] = run
            run = run + yu_r[d, s, i].astype(F32)

    def y_down(d, s):
        waits[d, s, 2]().wait_recv()
        base = jnp.zeros((DH // NY, DH), F32)
        for i in range(NZ):
            passed = i < z if d == 0 else i > z
            base = base + jnp.where(passed, z_r[d, s, i].astype(F32), 0.0)
        for i in range(NY):
            yd_s[d, s, i] = (base + ypre[d, s, i]).astype(BF16)
        scatter(yd_s.at[d, s], yd_r.at[d, s], d, s, 3, 1)
        yd_r[d, s, y] = yd_s[d, s, y]

    def x_down(d, s):
        waits[d, s, 3]().wait_recv()
        base = yd_r[d, s].reshape(DH, DH).astype(F32)
        for i in range(NX):
            xd_s[d, s, i] = (base + xpre[d, s, i]).astype(BF16)
        scatter(xd_s.at[d, s], xd_r.at[d, s], d, s, 4, 0)
        xd_r[d, s, x] = xd_s[d, s, x]

    def arrive(d, s):
        waits[d, s, 4]().wait_recv()
        for i in range(NX):
            second_state[d, s, i] = (xd_r[d, s, i].astype(F32) + first_term[d, s, i]).astype(BF16)

    def state(d, s, b, i):
        return xd_r[d, s, i] if b == order(d, NC)[0] else second_state[d, s, i]

    def local_forward(s, b):
        for i in range(NX):
            h = s * NX + i
            at = cols(h)
            sc = dot(q[b, :, at], k[b, :, at], 1, 1)
            wt = jnp.where(causal, sc, 0.0).astype(BF16)
            w[b, h] = wt
            local[b, :, at] = dot(wt, v[b, :, at], 1, 0)

    def normalize(s, b):
        for i in range(NX):
            at = cols(s * NX + i)
            a = local[b, :, at] + dot(q[b, :, at], state(0, s, b, i), 1, 0)
            inv = lax.rsqrt(jnp.mean(a * a, axis=-1, keepdims=True) + EPS)
            normed = a * inv
            att[b, :, at] = normed.astype(BF16)
            cot = g[b, :, at].astype(F32)
            m = jnp.mean(cot * normed, axis=-1, keepdims=True)
            da[b, :, at] = ((cot - normed * m) * inv).astype(BF16)

    def local_backward(s, b):
        for i in range(NX):
            h = s * NX + i
            at = cols(h)
            d_a = da[b, :, at]
            dw = jnp.where(causal, dot(d_a, v[b, :, at], 1, 1), 0.0).astype(BF16)
            gq[b, :, at] = (
                dot(dw, k[b, :, at], 1, 0) + dot(d_a, state(0, s, b, i), 1, 1)
            ).astype(BF16)
            gkl[b, :, at] = dot(dw, q[b, :, at], 0, 0)
            gvl[b, :, at] = dot(w[b, h], d_a, 0, 0)

    def finish(s, b):
        for i in range(NX):
            at = cols(s * NX + i)
            suf = state(1, s, b, i)
            gk[b, :, at] = (gkl[b, :, at] + dot(v[b, :, at], suf, 1, 1)).astype(BF16)
            gv[b, :, at] = (gvl[b, :, at] + dot(k[b, :, at], suf, 1, 0)).astype(BF16)

    leaving = []

    def leave(i, src, dst, s):
        pair = (
            far(i, src.at[peer, :, within(s)], dst.at[:, span(c, s)]),
            near(i, src.at[c, :, within(s)], dst.at[:, span(c, s)]),
        )
        for move in pair:
            move.start()
        leaving.append(pair)

    pl.semaphore_wait(barrier, 1 + (NX - 1) + (NY - 1) + (NZ - 1))
    for move in far_in:
        move.start()

    def ready(*which):
        for i in which:
            own_in[i].wait()
            far_in[i].wait_recv()

    ready(0, 1)
    x_up(0, 0)
    ready(2, 3)
    x_up(0, 1)
    ready(4, 5)
    middle = (y_up, z_all, y_down, x_down)
    work = [(s, b) for s in streams for b in range(NC)]
    local_forward(*work[0])
    for j, stage in enumerate(middle):
        for s in streams:
            stage(0, s)
        if j + 1 < len(work):
            local_forward(*work[j + 1])
    sent = list(pending)
    for s in streams:
        arrive(0, s)
        for b in range(NC):
            normalize(s, b)
        x_up(1, s)
    leave(6, att, att_out, None)
    local_backward(*work[0])
    for j, stage in enumerate(middle):
        for s in streams:
            stage(1, s)
        if j + 1 < len(work):
            local_backward(*work[j + 1])
    leave(7, gq, gq_out, None)
    for one in sent:
        one().wait_send()
        pending.remove(one)
    for move in far_in:
        move.wait_send()
    for s in streams:
        arrive(1, s)
        for b in range(NC):
            finish(s, b)
        leave(8 + 2 * s, gk, gk_out, s)
        leave(9 + 2 * s, gv, gv_out, s)
    for one in pending:
        one().wait_send()
    for away, home in leaving:
        home.wait()
        away.wait_send()
        away.wait_recv()


def hand_over(a, b, c, d, a_out, b_out, c_out, d_out, sem):
    copies = [
        pltpu.make_async_copy(src, dst, sem.at[i])
        for i, (src, dst) in enumerate(((a, a_out), (b, b_out), (c, c_out), (d, d_out)))
    ]
    for move in copies:
        move.start()
    for move in copies:
        move.wait()


def body(queries, key_rows, value_rows, grad_output):
    rows, feats = queries.shape
    half = feats // NC
    heads = half // DH
    per = (2, STREAMS)
    both = (NC, rows, half)
    chunk = DH // NY

    def vm(shape, dtype):
        return pltpu.VMEM(shape, dtype)

    square, strip = per + (NX, DH, DH), per + (NY, chunk, DH)
    scratch = (
        [vm(both, BF16)] * 4
        + [vm((NC, heads, rows, rows), BF16), vm(both, F32), vm(both, BF16)]
        + [vm(both, BF16)] * 4
        + [vm(both, F32)] * 2
        + [vm(square, F32), vm(square, BF16)]
        + [vm(square, BF16)] * 2
        + [vm(square, F32)]
        + [vm(strip, BF16)] * 2
        + [vm(strip, F32)]
        + [vm(per + (chunk, DH), BF16), vm(per + (NZ, chunk, DH), BF16)]
        + [vm(strip, BF16)] * 2
        + [vm(square, BF16)] * 2
        + [pltpu.SemaphoreType.DMA(per + (5,))] * 2
        + [pltpu.SemaphoreType.DMA((12,))] * 3
    )
    out = jax.ShapeDtypeStruct((rows, feats), BF16)
    results = pl.pallas_call(
        kernel,
        out_shape=(out,) * 4,
        in_specs=[pl.BlockSpec(memory_space=pltpu.HBM)] * 4,
        out_specs=(pl.BlockSpec(memory_space=pl.ANY),) * 4,
        scratch_shapes=scratch,
        compiler_params=pltpu.CompilerParams(
            collective_id=0, has_side_effects=True, vmem_limit_bytes=52864 * 1024
        ),
        cost_estimate=pl.CostEstimate(
            flops=24 * NC * heads * rows * DH * DH, bytes_accessed=16 * rows * feats,
            transcendentals=rows * NC * heads,
        ),
    )(queries, key_rows, value_rows, grad_output)
    return pl.pallas_call(
        hand_over,
        out_shape=(out,) * 4,
        in_specs=[pl.BlockSpec(memory_space=pl.ANY)] * 4,
        out_specs=(pl.BlockSpec(memory_space=pl.ANY),) * 4,
        scratch_shapes=[pltpu.SemaphoreType.DMA((4,))],
        compiler_params=pltpu.CompilerParams(vmem_limit_bytes=8 * 1024 * 1024),
    )(*results)


def solution(mesh):
    spec = P(("context", "tensor"), None)
    return jax.shard_map(
        body, mesh=mesh, in_specs=(spec,) * 4, out_specs=(spec,) * 4, check_vma=False
    )
```

```python
import jax
import jax.numpy as jnp
from jax import lax
from jax.experimental import pallas as pl
from jax.experimental.pallas import tpu as pltpu
from jax.sharding import PartitionSpec as P

DH = 128
NZ, NY, NX, NC = 8, 8, 4, 2
STREAMS = 2
UNROLL = 1
EPS = 1e-06
MESH = pl.DeviceIdType.MESH
F32 = jnp.float32
BF16 = jnp.bfloat16


def dot(a, b, ca, cb):
    return lax.dot_general(a, b, (((ca,), (cb,)), ((), ())), preferred_element_type=F32)


def kernel(
    q_in, k_in, v_in, g_in, att_out, gq_out, gk_out, gv_out,
    q, k, v, g, w, qt, local, da, att, gq, gk, gv, gkl, gvl,
    first_term, second_state, up_s, up_r, pre, z_s, z_r, down_s, down_r, ssem, rsem, own_sem, far_s, far_r,
):
    rows, half = q.shape[1], q.shape[2]
    part = half // STREAMS
    ctx, ten = lax.axis_index("context"), lax.axis_index("tensor")
    z, y = ctx // NY, lax.rem(ctx, NY)
    x, c = ten // NC, lax.rem(ten, NC)
    peer = 1 - c
    to_peer = (ctx, x * NC + peer)
    streams = range(STREAMS)

    def at_plane(i):
        return (z * NY + i // NX, lax.rem(i, NX) * NC + c)

    def at_z(i):
        return (i * NY + y, ten)

    def span(core, s):
        if s is None:
            return pl.ds(pl.multiple_of(core * half, half), half)
        return pl.ds(pl.multiple_of(core * half + s * part, part), part)

    def within(s):
        return pl.ds(0, half) if s is None else pl.ds(s * part, part)

    def near(i, src, dst):
        return pltpu.make_async_copy(src, dst, own_sem.at[i])

    def far(i, src, dst):
        return pltpu.make_async_remote_copy(
            src_ref=src, dst_ref=dst, send_sem=far_s.at[i], recv_sem=far_r.at[i],
            device_id=to_peer, device_id_type=MESH,
        )

    entering = [(k_in, k, 0), (v_in, v, 0), (k_in, k, 1), (v_in, v, 1), (q_in, q, None), (g_in, g, None)]
    own_in = [
        near(i, src.at[:, span(c, s)], dst.at[c, :, within(s)])
        for i, (src, dst, s) in enumerate(entering)
    ]
    far_in = [
        far(i, src.at[:, span(peer, s)], dst.at[c, :, within(s)])
        for i, (src, dst, s) in enumerate(entering)
    ]
    for move in own_in:
        move.start()

    plane = NY * NX
    rings = ((at_plane, y * NX + x, plane), (at_z, z, NZ))
    barrier = pltpu.get_barrier_semaphore()
    pl.semaphore_signal(barrier, inc=1, device_id=to_peer, device_id_type=MESH)
    for place, me, n in rings:
        for off in range(1, n):
            pl.semaphore_signal(
                barrier, inc=1, device_id=place(lax.rem(me + off, n)), device_id_type=MESH
            )

    row_id = lax.broadcasted_iota(jnp.int32, (rows, rows), 0)
    col_id = lax.broadcasted_iota(jnp.int32, (rows, rows), 1)
    causal = row_id >= col_id

    def cols(h):
        return pl.ds(pl.multiple_of(h * DH, DH), DH)

    def copy(src, dst, d, s, r, to):
        return pltpu.make_async_remote_copy(
            src_ref=src, dst_ref=dst, send_sem=ssem.at[d, s, r], recv_sem=rsem.at[d, s, r],
            device_id=to, device_id_type=MESH,
        )

    pending = []
    waits = {}

    def expect(dst, d, s, r, ring):
        place, me, n = rings[ring]

        def all_of():
            slots = dst.at[pl.ds(0, n - 1)]
            return copy(slots, slots, d, s, r, place(lax.rem(me + 1, n)))

        pending.append(all_of)
        waits[d, s, r] = all_of

    def scatter(src, dst, d, s, r, ring, whole=False):
        place, me, n = rings[ring]

        def send(off, _):
            to = lax.rem(me + off, n)
            copy(src if whole else src.at[to], dst.at[me], d, s, r, place(to)).start()
            return _

        lax.fori_loop(1, n, send, 0, unroll=UNROLL)
        expect(dst, d, s, r, ring)

    def order(d, n):
        return range(n) if d == 0 else range(n - 1, -1, -1)

    def term(d, b, h):
        if d == 0:
            return dot(k[b, :, cols(h)], v[b, :, cols(h)], 0, 0)
        return dot(qt[b, h], da[b, :, cols(h)], 1, 0)

    here = y * NX + x

    def up(d, s):
        for i in range(NX):
            ones = [term(d, b, s * NX + i) for b in order(d, NC)]
            total = (ones[0] + ones[1]).astype(BF16)
            up_s[d, s, i * NY : (i + 1) * NY] = total.reshape(NY, DH // NY, DH)
            first_term[d, s, i] = ones[0]
        scatter(up_s.at[d, s], up_r.at[d, s], d, s, 0, 0)
        up_r[d, s, here] = up_s[d, s, here]

    def z_all(d, s):
        waits[d, s, 0]().wait_recv()
        total = up_r[d, s, 0].astype(F32)
        for i in range(1, plane):
            total = total + up_r[d, s, i].astype(F32)
        z_s[d, s] = total.astype(BF16)
        scatter(z_s.at[d, s], z_r.at[d, s], d, s, 1, 1, whole=True)
        z_r[d, s, z] = z_s[d, s]
        run = jnp.zeros((DH // NY, DH), F32)
        for i in order(d, plane):
            pre[d, s, i] = run
            run = run + up_r[d, s, i].astype(F32)

    def down(d, s):
        waits[d, s, 1]().wait_recv()
        base = jnp.zeros((DH // NY, DH), F32)
        for i in range(NZ):
            passed = i < z if d == 0 else i > z
            base = base + jnp.where(passed, z_r[d, s, i].astype(F32), 0.0)
        for i in range(plane):
            down_s[d, s, i] = (base + pre[d, s, i]).astype(BF16)
        scatter(down_s.at[d, s], down_r.at[d, s], d, s, 2, 0)
        down_r[d, s, here] = down_s[d, s, here]

    def arrived(d, s, i):
        return down_r[d, s, i * NY : (i + 1) * NY].reshape(DH, DH)

    def arrive(d, s):
        waits[d, s, 2]().wait_recv()
        for i in range(NX):
            second_state[d, s, i] = (arrived(d, s, i).astype(F32) + first_term[d, s, i]).astype(BF16)

    def state(d, s, b, i):
        return arrived(d, s, i) if b == order(d, NC)[0] else second_state[d, s, i]

    def local_forward(s, b):
        for i in range(NX):
            h = s * NX + i
            at = cols(h)
            sc = dot(q[b, :, at], k[b, :, at], 1, 1)
            wt = jnp.where(causal, sc, 0.0).astype(BF16)
            w[b, h] = wt
            qt[b, h] = q[b, :, at].T
            local[b, :, at] = dot(wt, v[b, :, at], 1, 0)

    def normalize(s, b):
        for i in range(NX):
            at = cols(s * NX + i)
            a = local[b, :, at] + dot(q[b, :, at], state(0, s, b, i), 1, 0)
            inv = lax.rsqrt(jnp.mean(a * a, axis=-1, keepdims=True) + EPS)
            normed = a * inv
            att[b, :, at] = normed.astype(BF16)
            cot = g[b, :, at].astype(F32)
            m = jnp.mean(cot * normed, axis=-1, keepdims=True)
            da[b, :, at] = ((cot - normed * m) * inv).astype(BF16)

    def local_backward(s, b):
        for i in range(NX):
            h = s * NX + i
            at = cols(h)
            d_a = da[b, :, at]
            dw = jnp.where(causal, dot(d_a, v[b, :, at], 1, 1), 0.0).astype(BF16)
            gq[b, :, at] = (
                dot(dw, k[b, :, at], 1, 0) + dot(d_a, state(0, s, b, i), 1, 1)
            ).astype(BF16)
            gkl[b, :, at] = dot(dw, q[b, :, at], 0, 0)
            gvl[b, :, at] = dot(w[b, h], d_a, 0, 0)

    def finish(s, b):
        for i in range(NX):
            at = cols(s * NX + i)
            suf = state(1, s, b, i)
            gk[b, :, at] = (gkl[b, :, at] + dot(v[b, :, at], suf, 1, 1)).astype(BF16)
            gv[b, :, at] = (gvl[b, :, at] + dot(k[b, :, at], suf, 1, 0)).astype(BF16)

    leaving = []

    def leave(i, src, dst, s):
        pair = (
            far(i, src.at[peer, :, within(s)], dst.at[:, span(c, s)]),
            near(i, src.at[c, :, within(s)], dst.at[:, span(c, s)]),
        )
        for move in pair:
            move.start()
        leaving.append(pair)

    pl.semaphore_wait(barrier, 1 + (plane - 1) + (NZ - 1))
    for move in far_in:
        move.start()

    def ready(*which):
        for i in which:
            own_in[i].wait()
            far_in[i].wait_recv()

    ready(0, 1)
    up(0, 0)
    ready(2, 3)
    up(0, 1)
    ready(4, 5)
    middle = (z_all, down)
    work = [(s, b) for s in streams for b in range(NC)]
    for unit in work[:2]:
        local_forward(*unit)
    for j, stage in enumerate(middle):
        for s in streams:
            stage(0, s)
        for unit in work[2:] if j == 0 else ():
            local_forward(*unit)
    sent = list(pending)
    for s in streams:
        arrive(0, s)
        for b in range(NC):
            normalize(s, b)
        up(1, s)
    leave(6, att, att_out, None)
    for unit in work[:2]:
        local_backward(*unit)
    for j, stage in enumerate(middle):
        for s in streams:
            stage(1, s)
        for unit in work[2:] if j == 0 else ():
            local_backward(*unit)
    leave(7, gq, gq_out, None)
    for one in sent:
        one().wait_send()
        pending.remove(one)
    for move in far_in:
        move.wait_send()
    for s in streams:
        arrive(1, s)
        for b in range(NC):
            finish(s, b)
        leave(8 + 2 * s, gk, gk_out, s)
        leave(9 + 2 * s, gv, gv_out, s)
    for one in pending:
        one().wait_send()
    for away, home in leaving:
        home.wait()
        away.wait_send()
        away.wait_recv()


def hand_over(a, b, c, d, a_out, b_out, c_out, d_out, sem):
    copies = [
        pltpu.make_async_copy(src, dst, sem.at[i])
        for i, (src, dst) in enumerate(((a, a_out), (b, b_out), (c, c_out), (d, d_out)))
    ]
    for move in copies:
        move.start()
    for move in copies:
        move.wait()


def body(queries, key_rows, value_rows, grad_output):
    rows, feats = queries.shape
    half = feats // NC
    heads = half // DH
    per = (2, STREAMS)
    both = (NC, rows, half)
    chunk = DH // NY

    def vm(shape, dtype):
        return pltpu.VMEM(shape, dtype)

    square, strip = per + (NX, DH, DH), per + (NY * NX, chunk, DH)
    scratch = (
        [vm(both, BF16)] * 4
        + [vm((NC, heads, rows, rows), BF16), vm((NC, heads, DH, rows), BF16), vm(both, F32), vm(both, BF16)]
        + [vm(both, BF16)] * 4
        + [vm(both, F32)] * 2
        + [vm(square, F32), vm(square, BF16)]
        + [vm(strip, BF16)] * 2
        + [vm(strip, F32)]
        + [vm(per + (chunk, DH), BF16), vm(per + (NZ, chunk, DH), BF16)]
        + [vm(strip, BF16)] * 2
        + [pltpu.SemaphoreType.DMA(per + (3,))] * 2
        + [pltpu.SemaphoreType.DMA((12,))] * 3
    )
    out = jax.ShapeDtypeStruct((rows, feats), BF16)
    results = pl.pallas_call(
        kernel,
        out_shape=(out,) * 4,
        in_specs=[pl.BlockSpec(memory_space=pltpu.HBM)] * 4,
        out_specs=(pl.BlockSpec(memory_space=pl.ANY),) * 4,
        scratch_shapes=scratch,
        compiler_params=pltpu.CompilerParams(
            collective_id=0, has_side_effects=True, vmem_limit_bytes=52864 * 1024
        ),
        cost_estimate=pl.CostEstimate(
            flops=24 * NC * heads * rows * DH * DH, bytes_accessed=16 * rows * feats,
            transcendentals=rows * NC * heads,
        ),
    )(queries, key_rows, value_rows, grad_output)
    return pl.pallas_call(
        hand_over,
        out_shape=(out,) * 4,
        in_specs=[pl.BlockSpec(memory_space=pl.ANY)] * 4,
        out_specs=(pl.BlockSpec(memory_space=pl.ANY),) * 4,
        scratch_shapes=[pltpu.SemaphoreType.DMA((4,))],
        compiler_params=pltpu.CompilerParams(vmem_limit_bytes=8 * 1024 * 1024),
    )(*results)


def solution(mesh):
    spec = P(("context", "tensor"), None)
    return jax.shard_map(
        body, mesh=mesh, in_specs=(spec,) * 4, out_specs=(spec,) * 4, check_vma=False
    )
```

```python
import jax
import jax.numpy as jnp
from jax import lax
from jax.experimental import pallas as pl
from jax.experimental.pallas import tpu as pltpu
from jax.sharding import PartitionSpec as P

DH = 128
NZ, NY, NX, NC = 8, 8, 4, 2
STREAMS = 2
EPS = 1e-06
MESH = pl.DeviceIdType.MESH
F32 = jnp.float32
BF16 = jnp.bfloat16


def dot(a, b, ca, cb):
    return lax.dot_general(a, b, (((ca,), (cb,)), ((), ())), preferred_element_type=F32)


def kernel(
    q_in, k_in, v_in, g_in, att_out, gq_out, gk_out, gv_out,
    q, k, v, g, w, qt, local, da, att, gq, gk, gv, gkl, gvl,
    first_term, second_state, up_s, up_r, pre, z_s, z_r, down_s, down_r, ssem, rsem, own_sem, far_s, far_r,
):
    rows, half = q.shape[1], q.shape[2]
    part = half // STREAMS
    ctx, ten = lax.axis_index("context"), lax.axis_index("tensor")
    z, y = ctx // NY, lax.rem(ctx, NY)
    x, c = ten // NC, lax.rem(ten, NC)
    peer = 1 - c
    to_peer = (ctx, x * NC + peer)
    streams = range(STREAMS)

    def at_plane(i):
        return (z * NY + i // NX, lax.rem(i, NX) * NC + c)

    def at_z(i):
        return (i * NY + y, ten)

    def span(core, s):
        if s is None:
            return pl.ds(pl.multiple_of(core * half, half), half)
        return pl.ds(pl.multiple_of(core * half + s * part, part), part)

    def within(s):
        return pl.ds(0, half) if s is None else pl.ds(s * part, part)

    def near(i, src, dst):
        return pltpu.make_async_copy(src, dst, own_sem.at[i])

    def far(i, src, dst):
        return pltpu.make_async_remote_copy(
            src_ref=src, dst_ref=dst, send_sem=far_s.at[i], recv_sem=far_r.at[i],
            device_id=to_peer, device_id_type=MESH,
        )

    entering = [(k_in, k, 0), (v_in, v, 0), (k_in, k, 1), (v_in, v, 1), (q_in, q, None), (g_in, g, None)]
    own_in = [
        near(i, src.at[:, span(c, s)], dst.at[c, :, within(s)])
        for i, (src, dst, s) in enumerate(entering)
    ]
    far_in = [
        far(i, src.at[:, span(peer, s)], dst.at[c, :, within(s)])
        for i, (src, dst, s) in enumerate(entering)
    ]
    for move in own_in:
        move.start()

    plane = NY * NX
    rings = ((at_plane, y * NX + x, plane), (at_z, z, NZ))
    barrier = pltpu.get_barrier_semaphore()
    pl.semaphore_signal(barrier, inc=1, device_id=to_peer, device_id_type=MESH)
    for place, me, n in rings:
        for off in range(1, n):
            pl.semaphore_signal(
                barrier, inc=1, device_id=place(lax.rem(me + off, n)), device_id_type=MESH
            )

    row_id = lax.broadcasted_iota(jnp.int32, (rows, rows), 0)
    col_id = lax.broadcasted_iota(jnp.int32, (rows, rows), 1)
    causal = row_id >= col_id

    def hops(step, n):
        return min(step, n - step)

    steps = [(dy, dx) for dy in range(NY) for dx in range(NX) if (dy, dx) != (0, 0)]
    steps.sort(key=lambda step: -hops(step[0], NY) - hops(step[1], NX))
    targets = (
        [lax.rem(y + dy, NY) * NX + lax.rem(x + dx, NX) for dy, dx in steps],
        [lax.rem(z + dz, NZ) for dz in sorted(range(1, NZ), key=lambda dz: -hops(dz, NZ))],
    )

    def cols(h):
        return pl.ds(pl.multiple_of(h * DH, DH), DH)

    def copy(src, dst, d, s, r, to):
        return pltpu.make_async_remote_copy(
            src_ref=src, dst_ref=dst, send_sem=ssem.at[d, s, r], recv_sem=rsem.at[d, s, r],
            device_id=to, device_id_type=MESH,
        )

    pending = []
    waits = {}

    def expect(dst, d, s, r, ring):
        place, me, n = rings[ring]

        def all_of():
            slots = dst.at[pl.ds(0, n - 1)]
            return copy(slots, slots, d, s, r, place(lax.rem(me + 1, n)))

        pending.append(all_of)
        waits[d, s, r] = all_of

    def scatter(src, dst, d, s, r, ring, whole=False):
        place, me, n = rings[ring]
        for to in targets[ring]:
            copy(src if whole else src.at[to], dst.at[me], d, s, r, place(to)).start()
        expect(dst, d, s, r, ring)

    def order(d, n):
        return range(n) if d == 0 else range(n - 1, -1, -1)

    def term(d, b, h):
        if d == 0:
            return dot(k[b, :, cols(h)], v[b, :, cols(h)], 0, 0)
        return dot(qt[b, h], da[b, :, cols(h)], 1, 0)

    here = y * NX + x

    def up(d, s):
        for i in range(NX):
            ones = [term(d, b, s * NX + i) for b in order(d, NC)]
            total = (ones[0] + ones[1]).astype(BF16)
            up_s[d, s, i * NY : (i + 1) * NY] = total.reshape(NY, DH // NY, DH)
            first_term[d, s, i] = ones[0]
        scatter(up_s.at[d, s], up_r.at[d, s], d, s, 0, 0)
        up_r[d, s, here] = up_s[d, s, here]

    def z_all(d, s):
        waits[d, s, 0]().wait_recv()
        total = up_r[d, s, 0].astype(F32)
        for i in range(1, plane):
            total = total + up_r[d, s, i].astype(F32)
        z_s[d, s] = total.astype(BF16)
        scatter(z_s.at[d, s], z_r.at[d, s], d, s, 1, 1, whole=True)
        z_r[d, s, z] = z_s[d, s]
        run = jnp.zeros((DH // NY, DH), F32)
        for i in order(d, plane):
            pre[d, s, i] = run
            run = run + up_r[d, s, i].astype(F32)

    def down(d, s):
        waits[d, s, 1]().wait_recv()
        base = jnp.zeros((DH // NY, DH), F32)
        for i in range(NZ):
            passed = i < z if d == 0 else i > z
            base = base + jnp.where(passed, z_r[d, s, i].astype(F32), 0.0)
        for i in range(plane):
            down_s[d, s, i] = (base + pre[d, s, i]).astype(BF16)
        scatter(down_s.at[d, s], down_r.at[d, s], d, s, 2, 0)
        down_r[d, s, here] = down_s[d, s, here]

    def arrived(d, s, i):
        return down_r[d, s, i * NY : (i + 1) * NY].reshape(DH, DH)

    def arrive(d, s):
        waits[d, s, 2]().wait_recv()
        for i in range(NX):
            second_state[d, s, i] = (arrived(d, s, i).astype(F32) + first_term[d, s, i]).astype(BF16)

    def state(d, s, b, i):
        return arrived(d, s, i) if b == order(d, NC)[0] else second_state[d, s, i]

    def local_forward(s, b):
        for i in range(NX):
            h = s * NX + i
            at = cols(h)
            sc = dot(q[b, :, at], k[b, :, at], 1, 1)
            wt = jnp.where(causal, sc, 0.0).astype(BF16)
            w[b, h] = wt
            qt[b, h] = q[b, :, at].T
            local[b, :, at] = dot(wt, v[b, :, at], 1, 0)

    def normalize(s, b):
        for i in range(NX):
            at = cols(s * NX + i)
            a = local[b, :, at] + dot(q[b, :, at], state(0, s, b, i), 1, 0)
            inv = lax.rsqrt(jnp.mean(a * a, axis=-1, keepdims=True) + EPS)
            normed = a * inv
            att[b, :, at] = normed.astype(BF16)
            cot = g[b, :, at].astype(F32)
            m = jnp.mean(cot * normed, axis=-1, keepdims=True)
            da[b, :, at] = ((cot - normed * m) * inv).astype(BF16)

    def local_backward(s, b):
        for i in range(NX):
            h = s * NX + i
            at = cols(h)
            d_a = da[b, :, at]
            dw = jnp.where(causal, dot(d_a, v[b, :, at], 1, 1), 0.0).astype(BF16)
            gq[b, :, at] = (
                dot(dw, k[b, :, at], 1, 0) + dot(d_a, state(0, s, b, i), 1, 1)
            ).astype(BF16)
            gkl[b, :, at] = dot(dw, q[b, :, at], 0, 0)
            gvl[b, :, at] = dot(w[b, h], d_a, 0, 0)

    def finish(s, b):
        for i in range(NX):
            at = cols(s * NX + i)
            suf = state(1, s, b, i)
            gk[b, :, at] = (gkl[b, :, at] + dot(v[b, :, at], suf, 1, 1)).astype(BF16)
            gv[b, :, at] = (gvl[b, :, at] + dot(k[b, :, at], suf, 1, 0)).astype(BF16)

    leaving = []

    def leave(i, src, dst, s):
        pair = (
            far(i, src.at[peer, :, within(s)], dst.at[:, span(c, s)]),
            near(i, src.at[c, :, within(s)], dst.at[:, span(c, s)]),
        )
        for move in pair:
            move.start()
        leaving.append(pair)

    pl.semaphore_wait(barrier, 1 + (plane - 1) + (NZ - 1))
    for move in far_in:
        move.start()

    def ready(*which):
        for i in which:
            own_in[i].wait()
            far_in[i].wait_recv()

    ready(0, 1)
    up(0, 0)
    ready(2, 3)
    up(0, 1)
    ready(4, 5)
    middle = (z_all, down)
    work = [(s, b) for s in streams for b in range(NC)]
    for unit in work[:2]:
        local_forward(*unit)
    for j, stage in enumerate(middle):
        for s in streams:
            stage(0, s)
        for unit in work[2:] if j == 0 else ():
            local_forward(*unit)
    sent = list(pending)
    for s in streams:
        arrive(0, s)
        for b in range(NC):
            normalize(s, b)
        up(1, s)
    leave(6, att, att_out, None)
    for unit in work[:2]:
        local_backward(*unit)
    for j, stage in enumerate(middle):
        for s in streams:
            stage(1, s)
        for unit in work[2:] if j == 0 else ():
            local_backward(*unit)
    leave(7, gq, gq_out, None)
    for one in sent:
        one().wait_send()
        pending.remove(one)
    for move in far_in:
        move.wait_send()
    for s in streams:
        arrive(1, s)
        for b in range(NC):
            finish(s, b)
        leave(8 + 2 * s, gk, gk_out, s)
        leave(9 + 2 * s, gv, gv_out, s)
    for one in pending:
        one().wait_send()
    for away, home in leaving:
        home.wait()
        away.wait_send()
        away.wait_recv()


def hand_over(a, b, c, d, a_out, b_out, c_out, d_out, sem):
    copies = [
        pltpu.make_async_copy(src, dst, sem.at[i])
        for i, (src, dst) in enumerate(((a, a_out), (b, b_out), (c, c_out), (d, d_out)))
    ]
    for move in copies:
        move.start()
    for move in copies:
        move.wait()


def body(queries, key_rows, value_rows, grad_output):
    rows, feats = queries.shape
    half = feats // NC
    heads = half // DH
    per = (2, STREAMS)
    both = (NC, rows, half)
    chunk = DH // NY

    def vm(shape, dtype):
        return pltpu.VMEM(shape, dtype)

    square, strip = per + (NX, DH, DH), per + (NY * NX, chunk, DH)
    scratch = (
        [vm(both, BF16)] * 4
        + [vm((NC, heads, rows, rows), BF16), vm((NC, heads, DH, rows), BF16), vm(both, F32), vm(both, BF16)]
        + [vm(both, BF16)] * 4
        + [vm(both, F32)] * 2
        + [vm(square, F32), vm(square, BF16)]
        + [vm(strip, BF16)] * 2
        + [vm(strip, F32)]
        + [vm(per + (chunk, DH), BF16), vm(per + (NZ, chunk, DH), BF16)]
        + [vm(strip, BF16)] * 2
        + [pltpu.SemaphoreType.DMA(per + (3,))] * 2
        + [pltpu.SemaphoreType.DMA((12,))] * 3
    )
    out = jax.ShapeDtypeStruct((rows, feats), BF16)
    results = pl.pallas_call(
        kernel,
        out_shape=(out,) * 4,
        in_specs=[pl.BlockSpec(memory_space=pltpu.HBM)] * 4,
        out_specs=(pl.BlockSpec(memory_space=pl.ANY),) * 4,
        scratch_shapes=scratch,
        compiler_params=pltpu.CompilerParams(
            collective_id=0, has_side_effects=True, vmem_limit_bytes=52864 * 1024
        ),
        cost_estimate=pl.CostEstimate(
            flops=24 * NC * heads * rows * DH * DH, bytes_accessed=16 * rows * feats,
            transcendentals=rows * NC * heads,
        ),
    )(queries, key_rows, value_rows, grad_output)
    return pl.pallas_call(
        hand_over,
        out_shape=(out,) * 4,
        in_specs=[pl.BlockSpec(memory_space=pl.ANY)] * 4,
        out_specs=(pl.BlockSpec(memory_space=pl.ANY),) * 4,
        scratch_shapes=[pltpu.SemaphoreType.DMA((4,))],
        compiler_params=pltpu.CompilerParams(vmem_limit_bytes=8 * 1024 * 1024),
    )(*results)


def solution(mesh):
    spec = P(("context", "tensor"), None)
    return jax.shard_map(
        body, mesh=mesh, in_specs=(spec,) * 4, out_specs=(spec,) * 4, check_vma=False
    )
```
